32 devices in a mesh: seq: 8 (over z, x), sub: 4 (over y, core).
Axes of the slice: x: 2, y: 2, z: 4, core: 2. Of those that a mesh axis runs over, the one named last changes fastest.
Arguments:
- features: bfloat16 [32768, 768], P(('seq', 'sub')), may hold values from -6 to 6
- kernel: bfloat16 [3, 768, 384], replicated, may hold values from -0.125 to 0.125
- offsets: float32 [384], replicated, may hold values from -3 to 3
- mixer: bfloat16 [384, 768], replicated, may hold values from -0.3125 to 0.3125
- biases: float32 [768], replicated, may hold values from -3 to 3
- cotangent: bfloat16 [32768, 768], P(('seq', 'sub')), may hold values from -6 to 6
Outputs:
- layer_output: bfloat16 [32768, 768], P(('seq', 'sub'))
- input_grad: bfloat16 [32768, 768], P(('seq', 'sub'))
- kernel_grad: float32 [3, 768, 384], replicated
- offset_grad: float32 [384], replicated
- mixer_grad: float32 [384, 768], replicated
- biases_grad: float32 [768], replicated
The draws below stay inside these ranges and needn't reach their ends.
All inputs are finite; a program needn't handle non-finite values.
Results may differ from the reference program's by a relative error of at most 0.0075.
Values may be sent and summed in bfloat16 or wider, within the bound.
No kernel may reach another device: no remote copies, remote signals or barrier semaphores. Data moves between devices by JAX's collectives and lax.ppermute only.
A program may use at most 64 MiB of HBM per device.

```python
import math
import jax
import jax.numpy as jnp
from jax import lax

C = 768
H = 384
DILATION_STEP = 8192
LENGTH = 32768


def block_scale(rng, dims, split, smallest, high):
    level, own = 1.0, jax.random.fold_in(rng, 6)
    for axis_at, parts in split:
        heights = jnp.exp(jax.random.uniform(jax.random.fold_in(own, axis_at), (parts,), jnp.float32, smallest / len(split), high / len(split)))
        level = level * jnp.repeat(heights, dims[axis_at] // parts).reshape([-1 if axis == axis_at else 1 for axis in range(len(dims))])
    return level


def noise(own_key, shape, scale, most, pieces=(), held_as=jnp.bfloat16):
    gain = block_scale(own_key, shape, pieces, -0.22, 0.18) if pieces else 1.0
    drawn = jax.random.normal(own_key, shape, jnp.float32) * scale * gain
    return jnp.minimum(jnp.maximum(drawn, -most), most).astype(held_as)


def setup_inputs(seed: int = 0) -> dict:
    key_list = jax.random.split(jax.random.key(seed), 7)
    return {
        "features": noise(key_list[0], (LENGTH, C), 1.0, 6.0, ((0, 32),)),
        "kernel": noise(key_list[1], (3, C, H), (3 * C) ** -0.5, 0.125),
        "offsets": noise(key_list[2], (H,), 0.5, 3.0, (), jnp.float32),
        "mixer": noise(key_list[3], (H, C), H ** -0.5, 0.3125),
        "biases": noise(key_list[4], (C,), 0.5, 3.0, (), jnp.float32),
        "cotangent": noise(key_list[5], (LENGTH, C), 1.0, 6.0, ((0, 32),)),
    }


def gelu_exact(values):
    return jax.nn.gelu(values, approximate=False)

def gelu_slope(values):
    normal_cdf = 0.5 * (1.0 + jax.scipy.special.erf(values / math.sqrt(2.0)))
    return normal_cdf + values * jnp.exp(-0.5 * values * values) / math.sqrt(2.0 * math.pi)

def contract_rows(left, right):
    return jnp.dot(left.T, right, preferred_element_type=jnp.float32)

def reference(features, kernel, offsets, mixer, biases, cotangent):
    inputs = features.astype(jnp.float32)
    activated_output = gelu_exact(inputs).astype(jnp.bfloat16)
    behind_neighbor = jnp.roll(activated_output, DILATION_STEP, axis=0)
    ahead_neighbor = jnp.roll(activated_output, -DILATION_STEP, axis=0)
    tap_early = jnp.dot(behind_neighbor, kernel[0], preferred_element_type=jnp.float32).astype(jnp.bfloat16)
    tap_late = jnp.dot(ahead_neighbor, kernel[2], preferred_element_type=jnp.float32).astype(jnp.bfloat16)
    preact = jnp.dot(activated_output, kernel[1], preferred_element_type=jnp.float32) + tap_early.astype(jnp.float32) + tap_late.astype(jnp.float32) + offsets
    hidden = gelu_exact(preact).astype(jnp.bfloat16)
    layer_output = (inputs + jnp.dot(hidden, mixer, preferred_element_type=jnp.float32) + biases).astype(jnp.bfloat16)
    factor = 1.0 / math.sqrt(LENGTH)
    cot_float = cotangent.astype(jnp.float32)
    mixer_grad = contract_rows(hidden, cotangent) * factor
    biases_grad = lax.optimization_barrier(jnp.sum(cot_float, axis=0)) * factor
    hidden_grad = jnp.dot(cotangent, mixer.T, preferred_element_type=jnp.float32)
    preactivation_grad = (hidden_grad * gelu_slope(preact)).astype(jnp.bfloat16)
    kernel_grad = jnp.stack([contract_rows(behind_neighbor, preactivation_grad), contract_rows(activated_output, preactivation_grad), contract_rows(ahead_neighbor, preactivation_grad)]) * factor
    offset_grad = lax.optimization_barrier(jnp.sum(preactivation_grad.astype(jnp.float32), axis=0)) * factor
    activated_output_grad = jnp.dot(jnp.roll(preactivation_grad, -DILATION_STEP, axis=0), kernel[0].T, preferred_element_type=jnp.float32) + jnp.dot(preactivation_grad, kernel[1].T, preferred_element_type=jnp.float32) + jnp.dot(jnp.roll(preactivation_grad, DILATION_STEP, axis=0), kernel[2].T, preferred_element_type=jnp.float32)
    input_grad = (cot_float + activated_output_grad * gelu_slope(inputs)).astype(jnp.bfloat16)
    return (layer_output, input_grad, kernel_grad, offset_grad, mixer_grad, biases_grad)
```

```python
import math

import jax
import jax.numpy as jnp
from jax import lax
from jax.sharding import PartitionSpec as P

DILATION_STEP = 8192
AXES = ("seq", "sub")


def gelu_parts(values):
    normal_cdf = 0.5 * (1.0 + lax.erf(values * (1.0 / math.sqrt(2.0))))
    slope = normal_cdf + values * jnp.exp(-0.5 * values * values) * (1.0 / math.sqrt(2.0 * math.pi))
    return values * normal_cdf, slope


def contract_rows(left, right):
    return lax.dot_general(
        left, right, (((0,), (0,)), ((), ())), preferred_element_type=jnp.float32
    )


def times_transposed(left, right):
    return lax.dot_general(
        left, right, (((1,), (1,)), ((), ())), preferred_element_type=jnp.float32
    )


class Layout:
    def __init__(self, mesh_shape, rows):
        seq, sub = mesh_shape["seq"], mesh_shape["sub"]
        self.count = seq * sub
        self.plane = DILATION_STEP // rows
        self.ring = self.count // self.plane
        self.bins = rows * self.count

    def around(self, value, steps):
        hop = steps * self.plane
        pairs = [(i, (i + hop) % self.count) for i in range(self.count)]
        return lax.ppermute(value, AXES, pairs)

    def across(self, value, mask):
        return lax.ppermute(value, AXES, [(i, i ^ mask) for i in range(self.count)])

    def place(self):
        flat = lax.axis_index("seq") * lax.axis_size("sub") + lax.axis_index("sub")
        return flat % self.plane


def pick(stacked, index):
    return lax.dynamic_index_in_dim(stacked, index, 0, keepdims=False)


def encode(main, exact):
    parts = [main.astype(jnp.bfloat16)]
    if exact is not None:
        high = lax.reduce_precision(exact, 8, 7)
        low = lax.reduce_precision(exact - high, 8, 7)
        parts += [high.astype(jnp.bfloat16), low.astype(jnp.bfloat16)]
    return jnp.concatenate(parts, axis=-2) if len(parts) > 1 else parts[0]


def decode(sent, rows, extra):
    wide = sent.astype(jnp.float32)
    if not extra:
        return wide, None
    return wide[..., :rows, :], (
        wide[..., rows : rows + extra, :] + wide[..., rows + extra :, :]
    )


def plus(left, right):
    return left[0] + right[0], None if left[1] is None else left[1] + right[1]


def all_reduce(layout, main, exact):
    rows, extra = main.shape[1], 0 if exact is None else exact.shape[1]
    place = layout.place()
    core, block = place % 2, place // 2
    blocks = layout.plane // 2

    def cut(array, index):
        if array is None:
            return None
        return pick(array.reshape((blocks, 2) + array.shape[1:]).swapaxes(0, 1), index)

    arrived = layout.across(encode(cut(main, 1 - core), cut(exact, 1 - core)), 1)
    held = plus((cut(main, core), cut(exact, core)), decode(arrived, rows, extra))

    def one(index):
        return pick(held[0], index), None if exact is None else pick(held[1], index)

    arrived = [
        layout.across(encode(*one(block ^ k)), 2 * k) for k in range(1, blocks)
    ]
    total = one(block)
    for value in arrived:
        total = plus(total, decode(value, rows, extra))
    sent = encode(*total)
    level = [sent] + [layout.around(sent, -step) for step in range(1, layout.ring)]
    level = [decode(value, rows, extra) for value in level]
    while len(level) > 1:
        half = len(level) // 2
        level = [plus(level[i], level[i + half]) for i in range(half)]
    sent = encode(*level[0])
    gathered = jnp.zeros((blocks,) + sent.shape, sent.dtype)
    for k in range(blocks):
        value = sent if k == 0 else layout.across(sent, 2 * k)
        gathered = lax.dynamic_update_index_in_dim(gathered, value, block ^ k, 0)
    other = layout.across(gathered, 1)
    first = jnp.where(core == 0, gathered, other)
    second = jnp.where(core == 0, other, gathered)
    both = jnp.stack([first, second], axis=1).reshape((layout.plane,) + sent.shape)
    return decode(both, rows, extra)


def solution(mesh):
    mesh_shape = dict(mesh.shape)

    def local(features, kernel, offsets, mixer, biases, cotangent):
        rows, channels = features.shape
        width = kernel.shape[2]
        layout = Layout(mesh_shape, rows)
        factor = 1.0 / math.sqrt(layout.bins)
        plane = layout.plane
        cuts = [(0, 256), (256, width)]
        inputs = features.astype(jnp.float32)
        activated, slope_in = gelu_parts(inputs)
        activated = activated.astype(jnp.bfloat16)
        taps = []
        for low, high in cuts:
            early = jnp.dot(activated, kernel[0, :, low:high], preferred_element_type=jnp.float32)
            late = jnp.dot(activated, kernel[2, :, low:high], preferred_element_type=jnp.float32)
            taps.append(
                (
                    layout.around(early.astype(jnp.bfloat16), 1),
                    layout.around(late.astype(jnp.bfloat16), -1),
                )
            )
        center = jnp.dot(activated, kernel[1], preferred_element_type=jnp.float32)
        cot_float = cotangent.astype(jnp.float32)
        hidden_grad = times_transposed(cotangent, mixer)
        hidden, grads, arrived = [], [], []
        for (low, high), (early, late) in zip(cuts, taps):
            preact = (
                center[:, low:high]
                + early.astype(jnp.float32)
                + late.astype(jnp.float32)
                + offsets[low:high]
            )
            value, slope = gelu_parts(preact)
            hidden.append(value.astype(jnp.bfloat16))
            grad = (hidden_grad[:, low:high] * slope).astype(jnp.bfloat16)
            grads.append(grad)
            arrived.append((layout.around(grad, -1), layout.around(grad, 1)))
        hidden = jnp.concatenate(hidden, axis=1)
        grad = jnp.concatenate(grads, axis=1)
        layer_output = (
            inputs + jnp.dot(hidden, mixer, preferred_element_type=jnp.float32) + biases
        ).astype(jnp.bfloat16)
        mixer_part = contract_rows(cotangent, hidden) * factor
        center_part = contract_rows(activated, grad) * factor
        biases_part = jnp.sum(cot_float, axis=0) * factor
        offset_part = jnp.sum(grad.astype(jnp.float32), axis=0) * factor
        exact = jnp.concatenate([biases_part, offset_part]).reshape(plane, 1, -1)
        each = exact.shape[-1]
        exact = jnp.pad(exact, ((0, 0), (0, 7), (0, width - each)))
        first, vectors = all_reduce(
            layout,
            jnp.stack([center_part, mixer_part]).reshape(plane, -1, width),
            exact,
        )
        first = first.reshape(2, channels, width)
        vectors = vectors[:, 0, :each].reshape(-1)
        product = times_transposed(grad, kernel[1])
        sides = []
        for (low, high), (later, earlier) in zip(cuts, arrived):
            part = jnp.stack(
                [contract_rows(activated, later), contract_rows(activated, earlier)]
            ) * factor
            total, _ = all_reduce(layout, part.reshape(plane, -1, high - low), None)
            sides.append(total.reshape(2, channels, high - low))
            product = (
                product
                + times_transposed(later, kernel[0, :, low:high])
                + times_transposed(earlier, kernel[2, :, low:high])
            )
        input_grad = (cot_float + product * slope_in).astype(jnp.bfloat16)
        sides = jnp.concatenate(sides, axis=2)
        kernel_grad = jnp.stack([sides[0], first[0], sides[1]])
        mixer_grad = first[1].T
        return (
            layer_output,
            input_grad,
            kernel_grad,
            vectors[channels:],
            mixer_grad,
            vectors[:channels],
        )

    rows_split = P(AXES, None)
    return jax.shard_map(
        local,
        mesh=mesh,
        in_specs=(rows_split, P(), P(), P(), P(), rows_split),
        out_specs=(rows_split, rows_split, P(), P(), P(), P()),
        check_vma=False,
    )
```

```python
import math

import jax
import jax.numpy as jnp
from jax import lax
from jax.experimental import pallas as pl
from jax.experimental.pallas import tpu as pltpu
from jax.sharding import PartitionSpec as P

DILATION_STEP = 8192
AXES = ("seq", "sub")
VMEM_LIMIT = 32 * 1024 * 1024
BF16, F32 = jnp.bfloat16, jnp.float32


def gelu_parts(values):
    normal_cdf = 0.5 * (1.0 + lax.erf(values * (1.0 / math.sqrt(2.0))))
    slope = normal_cdf + values * jnp.exp(-0.5 * values * values) * (1.0 / math.sqrt(2.0 * math.pi))
    return values * normal_cdf, slope


def contract_rows(left, right):
    return lax.dot_general(
        left, right, (((0,), (0,)), ((), ())), preferred_element_type=jnp.float32
    )


def times_transposed(left, right):
    return lax.dot_general(
        left, right, (((1,), (1,)), ((), ())), preferred_element_type=jnp.float32
    )


class Chain:
    def __init__(self):
        self.last = ()

    def call(self, body, outs, operands, scratch=()):
        count, earlier = len(operands), self.last

        def kernel(*refs):
            body(*refs[:count], *refs[count + len(earlier) :])

        made = pl.pallas_call(
            kernel,
            out_shape=[jax.ShapeDtypeStruct(shape, dtype) for shape, dtype in outs],
            in_specs=[pl.BlockSpec(memory_space=pltpu.VMEM)] * count
            + [pl.BlockSpec(memory_space=pl.ANY)] * len(earlier),
            out_specs=[pl.BlockSpec(memory_space=pltpu.VMEM)] * len(outs),
            scratch_shapes=list(scratch),
            compiler_params=pltpu.CompilerParams(vmem_limit_bytes=VMEM_LIMIT),
            cost_estimate=pl.CostEstimate(flops=0, bytes_accessed=0, transcendentals=0),
        )(*operands, *earlier)
        self.last = (made[0],)
        return made


def blocks_of(rows, size=256):
    def run(body):
        def step(index, carry):
            body(pl.ds(pl.multiple_of(index * size, size), size))
            return carry

        lax.fori_loop(0, rows // size, step, 0)

    return run


def dot(left, right):
    return jnp.dot(left, right, preferred_element_type=jnp.float32)


class Layout:
    def __init__(self, mesh_shape, rows):
        seq, self.sub = mesh_shape["seq"], mesh_shape["sub"]
        self.count = seq * self.sub
        self.plane = DILATION_STEP // rows
        self.blocks = self.plane // 2
        self.ring = self.count // self.plane
        self.bins = rows * self.count

    def around(self, value, steps):
        hop = steps * self.plane
        pairs = [(i, (i + hop) % self.count) for i in range(self.count)]
        return lax.ppermute(value, AXES, pairs)

    def across(self, value, mask):
        return lax.ppermute(value, AXES, [(i, i ^ mask) for i in range(self.count)])

    def along(self, value, mask):
        return self.across(value, mask * self.plane)

    def place(self):
        flat = lax.axis_index("seq") * self.sub + lax.axis_index("sub")
        return flat & 1, lax.div(flat & (self.plane - 1), 2)


LANES, EXTRA = 128, 8


class Sum:
    def __init__(self, layout, channels, units, has_exact=False):
        self.layout, self.channels, self.units = layout, channels, units
        self.part = channels // layout.plane
        self.rows = self.part * units
        self.extra = EXTRA * has_exact
        self.held_type = ((layout.blocks, self.rows + self.extra, LANES), F32)
        self.sent_type = ((self.rows + 2 * self.extra, LANES), BF16)

    def store(self, ref, at, value):
        rows = self.rows
        if not self.extra:
            ref[at] = value.astype(BF16)
            return
        ref[at + (slice(0, rows),)] = value[:rows].astype(BF16)
        high = value[rows:].astype(BF16)
        low = (value[rows:] - high.astype(F32)).astype(BF16)
        ref[at + (slice(rows, None),)] = jnp.concatenate([high, low], axis=0)

    def load(self, value):
        value = value.astype(F32)
        if not self.extra:
            return value
        rows = self.rows
        exact = value[rows : rows + EXTRA] + value[rows + EXTRA :]
        return jnp.concatenate([value[:rows], exact], axis=0)

    def split(self, tall, wide, exact, held, away):
        core, _ = self.layout.place()
        part, plane = self.part, self.layout.plane
        thin = LANES // plane

        for block in range(self.layout.blocks):
            for mine in (True, False):
                piece = 2 * block + (core if mine else 1 - core)
                at = 0
                chunks = []
                for ref in tall:
                    for low in range(0, ref.shape[1], LANES):
                        chunks.append(ref[pl.ds(pl.multiple_of(piece * part, 8), part), low : low + LANES])
                for ref in wide:
                    for top in range(0, ref.shape[0], LANES):
                        for low in range(0, self.channels, LANES):
                            chunks.append(
                                ref[pl.ds(pl.multiple_of(top + piece * thin, 8), thin), low : low + LANES]
                            )
                if self.extra:
                    chunks.append(exact[pl.ds(pl.multiple_of(piece * EXTRA, 8), EXTRA), :])
                for value in chunks:
                    size = value.shape[0]
                    if mine:
                        held[block, at : at + size, :] = value
                    elif at < self.rows:
                        away[block, at : at + size, :] = value.astype(BF16)
                    else:
                        high = value.astype(BF16)
                        low = (value - high.astype(F32)).astype(BF16)
                        away[block, at : at + 2 * size, :] = jnp.concatenate([high, low], axis=0)
                    at += size


def sent_rows(sums):
    return sum(group.sent_type[0][0] for group in sums)


def over_plane(chain, layout, sums, halves):
    blocks, rows = layout.blocks, sent_rows(sums)

    def run(*refs):
        inputs, own, sent = refs[: 2 * len(sums)], refs[2 * len(sums)], refs[2 * len(sums) + 1 :]
        _, block = layout.place()
        top = base = 0
        for group, held, away in zip(sums, inputs[::2], inputs[1::2]):
            size, mine = group.sent_type[0][0], group.held_type[0][1]
            own[base : base + mine, :] = held[block] + group.load(away[block])
            for k in range(1, blocks):
                there = block ^ k
                group.store(sent[k - 1].at[top : top + size], (), held[there] + group.load(away[there]))
            top, base = top + size, base + mine

    mine = sum(group.held_type[0][1] for group in sums)
    outs = [((mine, LANES), F32)] + [((rows, LANES), BF16)] * (blocks - 1)
    own, *sent = chain.call(run, outs, [ref for pair in halves for ref in pair])
    return [own] + [layout.across(value, 2 * k) for k, value in enumerate(sent, 1)]


def plane_sum(chain, layout, sums, parts):
    def run(own, *refs):
        away, out = refs[:-1], refs[-1]
        top = base = 0
        for group in sums:
            size, mine = group.sent_type[0][0], group.held_type[0][1]
            value = own[base : base + mine, :]
            for ref in away:
                value = value + group.load(ref[top : top + size, :])
            group.store(out.at[top : top + size], (), value)
            top, base = top + size, base + mine

    return chain.call(run, [((sent_rows(sums), LANES), BF16)], parts)[0]


def pair_sum(chain, sums, mine, arrived):
    def run(left, right, out):
        top = 0
        for group in sums:
            size = group.sent_type[0][0]
            value = group.load(left[top : top + size, :]) + group.load(right[top : top + size, :])
            group.store(out.at[top : top + size], (), value)
            top += size

    return chain.call(run, [(mine.shape, BF16)], (mine, arrived))[0]


def back_plane(layout, sent):
    return [sent] + [layout.across(sent, 2 * k) for k in range(1, layout.blocks)]


def back_core(layout, own):
    return own + [layout.across(value, 1) for value in own]


def unsplit(layout, sums, refs, tall, wide, exact):
    core, block = layout.place()
    for at, ref in enumerate(refs):
        other, k = divmod(at, layout.blocks)
        piece = 2 * (block ^ k) + (core ^ other)
        top = 0
        for number, group in enumerate(sums):
            part = group.part
            for target, low in tall[number]:
                target[pl.ds(pl.multiple_of(piece * part, 8), part), low : low + LANES] = ref[
                    top : top + part, :
                ].astype(F32)
                top += part
            thin = LANES // layout.plane
            for target, upper in wide[number]:
                for low in range(0, group.channels, LANES):
                    target[pl.ds(pl.multiple_of(upper + piece * thin, 8), thin), low : low + LANES] = ref[
                        top : top + thin, :
                    ].astype(F32)
                    top += thin
            if group.extra:
                value = ref[top : top + 2 * EXTRA, :].astype(F32)
                exact[pl.ds(pl.multiple_of(piece * EXTRA, 8), EXTRA), :] = value[:EXTRA] + value[EXTRA:]
                top += 2 * EXTRA


def solution(mesh):
    mesh_shape = dict(mesh.shape)

    def local(features, kernel, offsets, mixer, biases, cotangent):
        rows, channels = features.shape
        width = kernel.shape[2]
        layout = Layout(mesh_shape, rows)
        factor = 1.0 / math.sqrt(layout.bins)
        plane = layout.plane
        cuts = [(0, 256), (256, width)]
        chain = Chain()

        def forward_taps(source, weights, early, late, activated):
            @blocks_of(rows)
            def _(block):
                active = gelu_parts(source[block, :].astype(F32))[0].astype(BF16)
                activated[block, :] = active
                early[block, :] = dot(active, weights[0]).astype(BF16)
                late[block, :] = dot(active, weights[2]).astype(BF16)

        early, late, activated = chain.call(
            forward_taps,
            [((rows, width), BF16)] * 2 + [((rows, channels), BF16)],
            (features, kernel),
        )
        early, late = layout.around(early, 1), layout.around(late, -1)

        def local_parts(active, weights, shift, cot, mix, center, hidden_grad):
            @blocks_of(rows)
            def _(block):
                center[block, :] = dot(active[block, :], weights[1]) + shift[...]
                hidden_grad[block, :] = times_transposed(cot[block, :], mix[...])

        center, hidden_grad = chain.call(
            local_parts,
            [((rows, width), F32)] * 2,
            (activated, kernel, offsets.reshape(1, width), cotangent, mixer),
        )

        def input_slope(source, slope):
            @blocks_of(rows)
            def _(block):
                slope[block, :] = gelu_parts(source[block, :].astype(F32))[1]

        (slope_in,) = chain.call(input_slope, [((rows, channels), F32)], (features,))

        def own_grads(low, high):
            def run(center, hidden_grad, early, late, hidden, grad):
                @blocks_of(rows)
                def _(block):
                    preact = (
                        center[block, low:high]
                        + early[block, low:high].astype(F32)
                        + late[block, low:high].astype(F32)
                    )
                    value, slope = gelu_parts(preact)
                    hidden[block, :] = value.astype(BF16)
                    grad[block, :] = (hidden_grad[block, low:high] * slope).astype(BF16)

            return run

        hidden, grads, arrived = [], [], []
        for low, high in cuts:
            outs = [((rows, high - low), BF16)] * 2
            value, grad = chain.call(own_grads(low, high), outs, (center, hidden_grad, early, late))
            hidden.append(value)
            grads.append(grad)
            arrived.append((layout.around(grad, -1), layout.around(grad, 1)))

        count = len(cuts)

        def vector_sums(cot, *refs):
            grads, out = refs[:-1], refs[-1]
            sources = [(cot, low) for low in range(0, channels, LANES)]
            sources += [(ref, low) for ref in grads for low in range(0, ref.shape[1], LANES)]
            out[...] = jnp.zeros_like(out)
            for row, (ref, low) in enumerate(sources):
                value = ref[:, low : low + LANES].astype(F32)
                out[row : row + 1, :] = jnp.sum(value, axis=0, keepdims=True) * factor

        (vectors,) = chain.call(vector_sums, [((plane * EXTRA, LANES), F32)], (cotangent, *grads))

        def split_types(group):
            shape, _ = group.held_type
            return [group.held_type, (shape[:1] + group.sent_type[0], BF16)]

        def own_weights(active, cot, exact, *refs):
            hidden, grads = refs[:count], refs[count : 2 * count]
            held, away, tall, wide = refs[2 * count :]
            for (low, high), value, grad in zip(cuts, hidden, grads):
                tall[:, low:high] = contract_rows(active[...], grad[...]) * factor
                wide[low:high, :] = contract_rows(value[...], cot[...]) * factor
            own.split([tall], [wide], exact, held, away)

        own_sums = [Sum(layout, channels, 2 * width // LANES, True)]
        own = own_sums[0]
        held, away = chain.call(
            own_weights,
            split_types(own),
            (activated, cotangent, vectors, *hidden, *grads),
            [pltpu.VMEM((channels, width), F32), pltpu.VMEM((width, channels), F32)],
        )

        own_half = (held, layout.across(away, 1))

        def output_parts(source, mix, shift, weights, *refs):
            hidden, grads = refs[:count], refs[count : 2 * count]
            output, product = refs[2 * count :]

            @blocks_of(rows)
            def _(block):
                total = source[block, :].astype(F32) + shift[...]
                back = jnp.zeros((total.shape[0], channels), F32)
                for (low, high), value, grad in zip(cuts, hidden, grads):
                    total = total + dot(value[block, :], mix[low:high, :])
                    back = back + times_transposed(grad[block, :], weights[1, :, low:high])
                output[block, :] = total.astype(BF16)
                product[block, :] = back

        layer_output, product = chain.call(
            output_parts,
            [((rows, channels), BF16), ((rows, channels), F32)],
            (features, mixer, biases.reshape(1, channels), kernel, *hidden, *grads),
        )

        def side_weights(group, low, high):
            def run(active, later, earlier, held, away, first, second):
                first[...] = contract_rows(active[...], later[...]) * factor
                second[...] = contract_rows(active[...], earlier[...]) * factor
                group.split([first, second], [], None, held, away)

            return run

        def side_product(low, high, is_last):
            def run(product, later, earlier, weights, *refs):
                @blocks_of(rows)
                def _(block):
                    total = (
                        product[block, :]
                        + times_transposed(later[block, :], weights[0, :, low:high])
                        + times_transposed(earlier[block, :], weights[2, :, low:high])
                    )
                    if is_last:
                        cot, slope, out = refs
                        total = cot[block, :].astype(F32) + total * slope[block, :]
                    else:
                        (out,) = refs
                    out[block, :] = total.astype(out.dtype)

            return run

        side_sums = [Sum(layout, channels, 2 * (high - low) // LANES) for low, high in cuts]

        def start_side(at):
            low, high = cuts[at]
            return chain.call(
                side_weights(side_sums[at], low, high),
                split_types(side_sums[at]),
                (activated, *arrived[at]),
                [pltpu.VMEM((channels, high - low), F32)] * 2,
            )

        def add_side(at, product):
            low, high = cuts[at]
            is_last = high == width
            return chain.call(
                side_product(low, high, is_last),
                [((rows, channels), BF16 if is_last else F32)],
                (product, *arrived[at], kernel) + ((cotangent, slope_in) if is_last else ()),
            )[0]

        held, away = start_side(0)
        halves = [(held, layout.across(away, 1))]
        own_parts = over_plane(chain, layout, own_sums, [own_half])
        product = add_side(0, product)
        held, away = start_side(1)
        own_sent = plane_sum(chain, layout, own_sums, own_parts)
        halves.append((held, layout.across(away, 1)))
        masks = [1 << bit for bit in range(layout.ring.bit_length() - 1)]
        arrived_own = layout.along(own_sent, masks[0])
        parts = over_plane(chain, layout, side_sums, halves)
        own_sent = pair_sum(chain, own_sums, own_sent, arrived_own)
        for mask in masks[1:-1]:
            own_sent = pair_sum(chain, own_sums, own_sent, layout.along(own_sent, mask))
        arrived_own = layout.along(own_sent, masks[-1])
        input_grad = add_side(count - 1, product)
        side_sent = plane_sum(chain, layout, side_sums, parts)
        arrived_side = layout.along(side_sent, masks[0])
        own_level = back_plane(layout, pair_sum(chain, own_sums, own_sent, arrived_own))
        side_sent = pair_sum(chain, side_sums, side_sent, arrived_side)
        for mask in masks[1:]:
            side_sent = pair_sum(chain, side_sums, side_sent, layout.along(side_sent, mask))
        side_level = back_core(layout, back_plane(layout, side_sent))
        own_level = back_core(layout, own_level)

        def finish(*refs):
            each = 2 * layout.blocks
            own_refs, side_refs = refs[:each], refs[each : 2 * each]
            kernel_grad, mixer_grad, exact = refs[2 * each :]
            units = [range(low, high, LANES) for low, high in cuts]
            unsplit(
                layout,
                own_sums,
                own_refs,
                [[(kernel_grad.at[1], low) for low in range(0, width, LANES)]],
                [[(mixer_grad, low) for low in range(0, width, LANES)]],
                exact,
            )
            unsplit(
                layout,
                side_sums,
                side_refs,
                [[(kernel_grad.at[i], low) for i in (0, 2) for low in unit] for unit in units],
                [[] for unit in units],
                None,
            )

        kernel_grad, mixer_grad, vectors = chain.call(
            finish,
            [
                ((3, channels, width), F32),
                ((width, channels), F32),
                ((plane * EXTRA, LANES), F32),
            ],
            (*own_level, *side_level),
        )
        vectors = vectors.reshape(-1)
        return (
            layer_output,
            input_grad,
            kernel_grad,
            vectors[channels : channels + width],
            mixer_grad,
            vectors[:channels],
        )

    rows_split = P(AXES, None)
    return jax.shard_map(
        local,
        mesh=mesh,
        in_specs=(rows_split, P(), P(), P(), P(), rows_split),
        out_specs=(rows_split, rows_split, P(), P(), P(), P()),
        check_vma=False,
    )
```

```python
import math

import jax
import jax.numpy as jnp
from jax import lax
from jax.experimental import pallas as pl
from jax.experimental.pallas import tpu as pltpu
from jax.sharding import PartitionSpec as P

DILATION_STEP = 8192
AXES = ("seq", "sub")
VMEM_LIMIT = 16 * 1024 * 1024
LONG = 8 * 10**9
BF16, F32 = jnp.bfloat16, jnp.float32


def gelu_parts(values):
    normal_cdf = 0.5 * (1.0 + lax.erf(values * (1.0 / math.sqrt(2.0))))
    slope = normal_cdf + values * jnp.exp(-0.5 * values * values) * (1.0 / math.sqrt(2.0 * math.pi))
    return values * normal_cdf, slope


def contract_rows(left, right):
    return lax.dot_general(
        left, right, (((0,), (0,)), ((), ())), preferred_element_type=jnp.float32
    )


def times_transposed(left, right):
    return lax.dot_general(
        left, right, (((1,), (1,)), ((), ())), preferred_element_type=jnp.float32
    )


class Chain:
    def __init__(self):
        self.last = ()

    def call(self, body, outs, operands, scratch=(), flops=0, blocked=(), key=0, far=(), alias=False):
        count, earlier = len(operands), self.last

        def kernel(*refs):
            body(*refs[:count], *refs[count + len(earlier) :])

        def spec(shape, at):
            if at in far:
                return pl.BlockSpec(memory_space=pltpu.HBM)
            if not blocked:
                return pl.BlockSpec(memory_space=pltpu.VMEM)
            if blocked[at]:
                return pl.BlockSpec((shape[0] // 4,) + shape[1:], lambda i: (i, 0))
            return pl.BlockSpec(shape, lambda i: (0,) * len(shape))

        made = pl.pallas_call(
            kernel,
            grid=(4,) if blocked else (),
            out_shape=[jax.ShapeDtypeStruct(shape, dtype) for shape, dtype in outs],
            in_specs=[spec(value.shape, at) for at, value in enumerate(operands)]
            + [pl.BlockSpec(memory_space=pl.ANY)] * len(earlier),
            out_specs=[spec(shape, count + at) for at, (shape, _) in enumerate(outs)],
            scratch_shapes=list(scratch),
            input_output_aliases={0: 0} if alias else {},
            compiler_params=pltpu.CompilerParams(vmem_limit_bytes=VMEM_LIMIT),
            cost_estimate=pl.CostEstimate(flops=flops, bytes_accessed=0, transcendentals=0),
        )(*operands, *earlier)
        self.last = (made[key],)
        return made


def blocks_of(rows, size=256):
    def run(body):
        def step(index, carry):
            body(pl.ds(pl.multiple_of(index * size, size), size))
            return carry

        lax.fori_loop(0, rows // size, step, 0)

    return run


def dot(left, right):
    return jnp.dot(left, right, preferred_element_type=jnp.float32)


class Layout:
    def __init__(self, mesh_shape, rows):
        seq, self.sub = mesh_shape["seq"], mesh_shape["sub"]
        self.count = seq * self.sub
        self.plane = DILATION_STEP // rows
        self.blocks = self.plane // 2
        self.ring = self.count // self.plane
        self.bins = rows * self.count

    def around(self, value, steps):
        hop = steps * self.plane
        pairs = [(i, (i + hop) % self.count) for i in range(self.count)]
        return lax.ppermute(value, AXES, pairs)

    def across(self, value, mask):
        return lax.ppermute(value, AXES, [(i, i ^ mask) for i in range(self.count)])

    def along(self, value, mask):
        return self.across(value, mask * self.plane)

    def place(self):
        flat = lax.axis_index("seq") * self.sub + lax.axis_index("sub")
        return flat & 1, lax.div(flat & (self.plane - 1), 2)


LANES, EXTRA = 128, 8


class Sum:
    def __init__(self, layout, channels, units, has_exact=False):
        self.layout, self.channels, self.units = layout, channels, units
        self.part = channels // layout.plane
        self.rows = self.part * units
        self.extra = EXTRA * has_exact
        self.held_type = ((layout.blocks, self.rows + self.extra, LANES), F32)
        self.sent_type = ((self.rows + 2 * self.extra, LANES), BF16)

    def store(self, ref, at, value):
        rows = self.rows
        if not self.extra:
            ref[at] = value.astype(BF16)
            return
        ref[at + (slice(0, rows),)] = value[:rows].astype(BF16)
        high = value[rows:].astype(BF16)
        low = (value[rows:] - high.astype(F32)).astype(BF16)
        ref[at + (slice(rows, None),)] = jnp.concatenate([high, low], axis=0)

    def load(self, value):
        value = value.astype(F32)
        if not self.extra:
            return value
        rows = self.rows
        exact = value[rows : rows + EXTRA] + value[rows + EXTRA :]
        return jnp.concatenate([value[:rows], exact], axis=0)

    def split(self, tall, wide, exact, held, away):
        core, _ = self.layout.place()
        part, plane = self.part, self.layout.plane
        thin = LANES // plane

        for block in range(self.layout.blocks):
            for mine in (True, False):
                piece = 2 * block + (core if mine else 1 - core)
                at = 0
                chunks = []
                for ref in tall:
                    for low in range(0, ref.shape[1], LANES):
                        chunks.append(ref[pl.ds(pl.multiple_of(piece * part, 8), part), low : low + LANES])
                for ref in wide:
                    for top in range(0, ref.shape[0], LANES):
                        for low in range(0, self.channels, LANES):
                            chunks.append(
                                ref[pl.ds(pl.multiple_of(top + piece * thin, 8), thin), low : low + LANES]
                            )
                if self.extra:
                    chunks.append(exact[pl.ds(pl.multiple_of(piece * EXTRA, 8), EXTRA), :])
                for value in chunks:
                    size = value.shape[0]
                    if mine:
                        held[block, at : at + size, :] = value
                    elif at < self.rows:
                        away[block, at : at + size, :] = value.astype(BF16)
                    else:
                        high = value.astype(BF16)
                        low = (value - high.astype(F32)).astype(BF16)
                        away[block, at : at + 2 * size, :] = jnp.concatenate([high, low], axis=0)
                    at += size


def sent_rows(sums):
    return sum(group.sent_type[0][0] for group in sums)


def over_plane(chain, layout, sums, halves):
    blocks, rows = layout.blocks, sent_rows(sums)

    def run(*refs):
        inputs, own, sent = refs[: 2 * len(sums)], refs[2 * len(sums)], refs[2 * len(sums) + 1 :]
        _, block = layout.place()
        top = base = 0
        for group, held, away in zip(sums, inputs[::2], inputs[1::2]):
            size, mine = group.sent_type[0][0], group.held_type[0][1]
            own[base : base + mine, :] = held[block] + group.load(away[block])
            for k in range(1, blocks):
                there = block ^ k
                group.store(sent[k - 1].at[top : top + size], (), held[there] + group.load(away[there]))
            top, base = top + size, base + mine

    mine = sum(group.held_type[0][1] for group in sums)
    outs = [((mine, LANES), F32)] + [((rows, LANES), BF16)] * (blocks - 1)
    own, *sent = chain.call(run, outs, [ref for pair in halves for ref in pair])
    return [own] + [layout.across(value, 2 * k) for k, value in enumerate(sent, 1)]


def plane_sum(chain, layout, sums, parts, flops=0):
    def run(own, *refs):
        away, out = refs[:-1], refs[-1]
        top = base = 0
        for group in sums:
            size, mine = group.sent_type[0][0], group.held_type[0][1]
            value = own[base : base + mine, :]
            for ref in away:
                value = value + group.load(ref[top : top + size, :])
            group.store(out.at[top : top + size], (), value)
            top, base = top + size, base + mine

    return chain.call(run, [((sent_rows(sums), LANES), BF16)], parts, flops=flops)[0]


def pair_sum(chain, sums, mine, arrived, flops=0):
    def run(left, right, out):
        top = 0
        for group in sums:
            size = group.sent_type[0][0]
            value = group.load(left[top : top + size, :]) + group.load(right[top : top + size, :])
            group.store(out.at[top : top + size], (), value)
            top += size

    return chain.call(run, [(mine.shape, BF16)], (mine, arrived), flops=flops)[0]


def back_plane(layout, sent):
    return [sent] + [layout.across(sent, 2 * k) for k in range(1, layout.blocks)]


def back_core(chain, layout, parts, flops=0):
    def run(*refs):
        for at, ref in enumerate(refs[:-1]):
            refs[-1][at] = ref[...]

    (own,) = chain.call(run, [((len(parts),) + parts[0].shape, BF16)], parts, flops=flops)
    return own, layout.across(own, 1)


def unsplit(layout, sums, refs, tall, wide, exact):
    core, block = layout.place()
    for at in range(2 * layout.blocks):
        other, k = divmod(at, layout.blocks)
        ref = refs[other].at[k]
        piece = 2 * (block ^ k) + (core ^ other)
        top = 0
        for number, group in enumerate(sums):
            part = group.part
            for target, low in tall[number]:
                target[pl.ds(pl.multiple_of(piece * part, 8), part), low : low + LANES] = ref[
                    top : top + part, :
                ].astype(F32)
                top += part
            thin = LANES // layout.plane
            for target, upper in wide[number]:
                for low in range(0, group.channels, LANES):
                    target[pl.ds(pl.multiple_of(upper + piece * thin, 8), thin), low : low + LANES] = ref[
                        top : top + thin, :
                    ].astype(F32)
                    top += thin
            if group.extra:
                value = ref[top : top + 2 * EXTRA, :].astype(F32)
                exact[pl.ds(pl.multiple_of(piece * EXTRA, 8), EXTRA), :] = value[:EXTRA] + value[EXTRA:]
                top += 2 * EXTRA


def solution(mesh):
    mesh_shape = dict(mesh.shape)

    def local(features, kernel, offsets, mixer, biases, cotangent):
        rows, channels = features.shape
        width = kernel.shape[2]
        layout = Layout(mesh_shape, rows)
        factor = 1.0 / math.sqrt(layout.bins)
        plane = layout.plane
        cuts = [(0, LANES), (LANES, width)]
        chain = Chain()

        def forward_taps(source, weights, early, late, activated):
            @blocks_of(rows)
            def _(block):
                active = gelu_parts(source[block, :].astype(F32))[0].astype(BF16)
                activated[block, :] = active
                early[block, :] = dot(active, weights[0]).astype(BF16)
                late[block, :] = dot(active, weights[2]).astype(BF16)

        early, late, activated = chain.call(
            forward_taps,
            [((rows, width), BF16)] * 2 + [((rows, channels), BF16)],
            (features, kernel),
        )
        early, late = layout.around(early, 1), layout.around(late, -1)

        def local_parts(active, weights, shift, cot, mix, center, hidden_grad):
            @blocks_of(rows)
            def _(block):
                center[block, :] = dot(active[block, :], weights[1]) + shift[...]
                hidden_grad[block, :] = times_transposed(cot[block, :], mix[...])

        center, hidden_grad = chain.call(
            local_parts,
            [((rows, width), F32)] * 2,
            (activated, kernel, offsets.reshape(1, width), cotangent, mixer),
        )

        def own_grads(low, high):
            def run(center, hidden_grad, early, late, hidden, grad):
                @blocks_of(rows)
                def _(block):
                    preact = (
                        center[block, low:high]
                        + early[block, low:high].astype(F32)
                        + late[block, low:high].astype(F32)
                    )
                    value, slope = gelu_parts(preact)
                    hidden[block, :] = value.astype(BF16)
                    grad[block, :] = (hidden_grad[block, low:high] * slope).astype(BF16)

            return run

        hidden, grads, arrived = [], [], []
        for low, high in cuts:
            outs = [((rows, high - low), BF16)] * 2
            value, grad = chain.call(own_grads(low, high), outs, (center, hidden_grad, early, late))
            hidden.append(value)
            grads.append(grad)
            arrived.append((layout.around(grad, -1), layout.around(grad, 1)))

        count = len(cuts)

        def vector_sums(cot, *refs):
            grads, out = refs[:-1], refs[-1]
            sources = [(cot, low) for low in range(0, channels, LANES)]
            sources += [(ref, low) for ref in grads for low in range(0, ref.shape[1], LANES)]
            out[...] = jnp.zeros_like(out)
            for row, (ref, low) in enumerate(sources):
                value = ref[:, low : low + LANES].astype(F32)
                out[row : row + 1, :] = jnp.sum(value, axis=0, keepdims=True) * factor

        (vectors,) = chain.call(vector_sums, [((plane * EXTRA, LANES), F32)], (cotangent, *grads))

        def split_types(group):
            shape, _ = group.held_type
            return [group.held_type, (shape[:1] + group.sent_type[0], BF16)]

        def own_weights(active, cot, exact, *refs):
            hidden, grads = refs[:count], refs[count : 2 * count]
            held, away, tall, wide = refs[2 * count :]
            for (low, high), value, grad in zip(cuts, hidden, grads):
                tall[:, low:high] = contract_rows(active[...], grad[...]) * factor
                wide[low:high, :] = contract_rows(value[...], cot[...]) * factor
            own.split([tall], [wide], exact, held, away)

        own = Sum(layout, channels, 2 * width // LANES, True)
        held, away = chain.call(
            own_weights,
            split_types(own),
            (activated, cotangent, vectors, *hidden, *grads),
            [pltpu.VMEM((channels, width), F32), pltpu.VMEM((width, channels), F32)],
        )

        own_half = (held, layout.across(away, 1))

        def output_parts(source, mix, shift, weights, *refs):
            hidden, grads = refs[:count], refs[count : 2 * count]
            output, product = refs[2 * count :]

            @blocks_of(rows)
            def _(block):
                total = source[block, :].astype(F32) + shift[...]
                back = jnp.zeros((total.shape[0], channels), F32)
                for (low, high), value, grad in zip(cuts, hidden, grads):
                    total = total + dot(value[block, :], mix[low:high, :])
                    back = back + times_transposed(grad[block, :], weights[1, :, low:high])
                output[block, :] = total.astype(BF16)
                product[block, :] = back

        layer_output, product = chain.call(
            output_parts,
            [((rows, channels), BF16), ((rows, channels), F32)],
            (features, mixer, biases.reshape(1, channels), kernel, *hidden, *grads),
            flops=LONG,
            key=1,
        )

        def side_weights(group, low, high):
            def run(active, later, earlier, held, away, first, second):
                first[...] = contract_rows(active[...], later[...]) * factor
                second[...] = contract_rows(active[...], earlier[...]) * factor
                group.split([first, second], [], None, held, away)

            return run

        def side_product(product, later, earlier, weights, out):
            low, high = cuts[0]

            @blocks_of(rows)
            def _(block):
                out[block, :] = (
                    product[block, :]
                    + times_transposed(later[block, :], weights[0, :, low:high])
                    + times_transposed(earlier[block, :], weights[2, :, low:high])
                )

        def input_grads(product, later, earlier, weights, cot, slope, out, done):
            low, high = cuts[1]
            done[...] = jnp.zeros_like(done)

            @blocks_of(rows)
            def _(block):
                total = (
                    product[block, :]
                    + times_transposed(later[block, :], weights[0, :, low:high])
                    + times_transposed(earlier[block, :], weights[2, :, low:high])
                )
                out[block, :] = (cot[block, :].astype(F32) + total * slope[block, :]).astype(BF16)

        side_sums = [Sum(layout, channels, 2 * (high - low) // LANES) for low, high in cuts]

        FLOPS = (LONG, LONG)

        def start_side(at):
            low, high = cuts[at]
            return chain.call(
                side_weights(side_sums[at], low, high),
                split_types(side_sums[at]),
                (activated, *arrived[at]),
                [pltpu.VMEM((channels, high - low), F32)] * 2,
                FLOPS[at],
            )

        def input_slope(source, slope):
            @blocks_of(rows)
            def _(block):
                slope[block, :] = gelu_parts(source[block, :].astype(F32))[1]


        held, away = start_side(0)
        halves = [own_half, (held, layout.across(away, 1))]
        (product,) = chain.call(
            side_product,
            [((rows, channels), F32)],
            (product, *arrived[0], kernel),
            flops=LONG,
        )
        first_sums, last_sums = [own, side_sums[0]], side_sums[1:]
        parts = over_plane(chain, layout, first_sums, halves)
        (slope_in,) = chain.call(input_slope, [((rows, channels), F32)], (features,), flops=LONG)
        first_sent = plane_sum(chain, layout, first_sums, parts, LONG)
        masks = [1 << bit for bit in range(layout.ring.bit_length() - 1)]
        first_arrived = layout.along(first_sent, masks[0])

        held, away = start_side(1)
        halves = [(held, layout.across(away, 1))]
        for mask in masks[1:]:
            first_sent = pair_sum(chain, first_sums, first_sent, first_arrived, LONG)
            first_arrived = layout.along(first_sent, mask)
        parts = over_plane(chain, layout, last_sums, halves)
        last_sent = plane_sum(chain, layout, last_sums, parts)
        last_arrived = layout.along(last_sent, masks[0])
        first_level = back_plane(layout, pair_sum(chain, first_sums, first_sent, first_arrived))
        for mask in masks[1:]:
            last_sent = pair_sum(chain, last_sums, last_sent, last_arrived)
            last_arrived = layout.along(last_sent, mask)
        input_grad, _ = chain.call(
            input_grads,
            [((rows, channels), BF16), ((8, LANES), F32)],
            (product, *arrived[1], kernel, cotangent, slope_in),
            flops=LONG,
            key=1,
        )
        last_sent = pair_sum(chain, last_sums, last_sent, last_arrived)
        last_level = back_plane(layout, last_sent)
        first_level = back_core(chain, layout, first_level, LONG)
        last_level = back_core(chain, layout, last_level, LONG)

        def side_targets(kernel_grad, low, high):
            return [(kernel_grad.at[i], at) for i in (0, 2) for at in range(low, high, LANES)]

        def finish_first(*refs):
            arrived, refs = refs[:2], refs[2:]
            kernel_grad, mixer_grad, biases_grad, offset_grad = refs[:4]
            center, sides, exact, sems = refs[4:]
            targets = range(0, width, LANES)
            low, high = cuts[0]
            unsplit(
                layout,
                first_sums,
                arrived,
                [
                    [(center, at) for at in targets],
                    [(sides.at[i], at) for i in (0, 1) for at in range(0, high - low, LANES)],
                ],
                [[(mixer_grad, at) for at in targets], []],
                exact,
            )
            copies = [pltpu.make_async_copy(center, kernel_grad.at[1], sems.at[0])]
            for i in (0, 1):
                copies.append(
                    pltpu.make_async_copy(
                        sides.at[i], kernel_grad.at[2 * i, :, low:high], sems.at[1 + i]
                    )
                )
            for copy in copies:
                copy.start()
            for at in range(0, channels, LANES):
                biases_grad[at : at + LANES] = exact[at // LANES, :]
            for at in range(0, width, LANES):
                offset_grad[at : at + LANES] = exact[(channels + at) // LANES, :]
            for copy in copies:
                copy.wait()

        low, high = cuts[0]
        kernel_grad, mixer_grad, biases_grad, offset_grad = chain.call(
            finish_first,
            [
                ((3, channels, width), F32),
                ((width, channels), F32),
                ((channels,), F32),
                ((width,), F32),
            ],
            first_level,
            [
                pltpu.VMEM((channels, width), F32),
                pltpu.VMEM((2, channels, high - low), F32),
                pltpu.VMEM((plane * EXTRA, LANES), F32),
                pltpu.SemaphoreType.DMA((3,)),
            ],
            far=(2,),
            key=3,
        )

        def finish_last(begun, *refs):
            arrived, (kernel_grad, sides, sems) = refs[:2], refs[2:]
            low, high = cuts[1]
            unsplit(
                layout,
                last_sums,
                arrived,
                [[(sides.at[i], at) for i in (0, 1) for at in range(0, high - low, LANES)]],
                [[]],
                None,
            )
            copies = [
                pltpu.make_async_copy(sides.at[i], kernel_grad.at[2 * i, :, low:high], sems.at[i])
                for i in (0, 1)
            ]
            for copy in copies:
                copy.start()
            for copy in copies:
                copy.wait()

        low, high = cuts[1]
        chain.last = ()
        (kernel_grad,) = chain.call(
            finish_last,
            [((3, channels, width), F32)],
            (kernel_grad, *last_level),
            [pltpu.VMEM((2, channels, high - low), F32), pltpu.SemaphoreType.DMA((2,))],
            far=(0, 3),
            alias=True,
        )
        return (
            layer_output,
            input_grad,
            kernel_grad,
            offset_grad,
            mixer_grad,
            biases_grad,
        )

    rows_split = P(AXES, None)
    return jax.shard_map(
        local,
        mesh=mesh,
        in_specs=(rows_split, P(), P(), P(), P(), rows_split),
        out_specs=(rows_split, rows_split, P(), P(), P(), P()),
        check_vma=False,
    )
```

```python
import math

import jax
import jax.numpy as jnp
from jax import lax
from jax.experimental import pallas as pl
from jax.experimental.pallas import tpu as pltpu
from jax.sharding import PartitionSpec as P

DILATION_STEP = 8192
AXES = ("seq", "sub")
VMEM_LIMIT = 16 * 1024 * 1024
LONG = 8 * 10**9
BF16, F32 = jnp.bfloat16, jnp.float32


def gelu_parts(values):
    normal_cdf = 0.5 * (1.0 + lax.erf(values * (1.0 / math.sqrt(2.0))))
    slope = normal_cdf + values * jnp.exp(-0.5 * values * values) * (1.0 / math.sqrt(2.0 * math.pi))
    return values * normal_cdf, slope


def contract_rows(left, right):
    return lax.dot_general(
        left, right, (((0,), (0,)), ((), ())), preferred_element_type=jnp.float32
    )


def times_transposed(left, right):
    return lax.dot_general(
        left, right, (((1,), (1,)), ((), ())), preferred_element_type=jnp.float32
    )


class Chain:
    def __init__(self):
        self.last = ()

    def call(self, body, outs, operands, scratch=(), flops=0, blocked=(), key=0, far=(), alias=False, tap=None):
        count, earlier = len(operands), self.last

        def kernel(*refs):
            body(*refs[:count], *refs[count + len(earlier) :])

        def spec(shape, at):
            if tap is not None and at == count - 1:
                return pl.BlockSpec((1,) + shape[1:], lambda _: (tap, 0, 0))
            if at in far:
                return pl.BlockSpec(memory_space=pltpu.HBM)
            if not blocked:
                return pl.BlockSpec(memory_space=pltpu.VMEM)
            if blocked[at]:
                return pl.BlockSpec((shape[0] // 4,) + shape[1:], lambda i: (i, 0))
            return pl.BlockSpec(shape, lambda i: (0,) * len(shape))

        made = pl.pallas_call(
            kernel,
            grid=(4,) if blocked else () if tap is None else (1,),
            out_shape=[jax.ShapeDtypeStruct(shape, dtype) for shape, dtype in outs],
            in_specs=[spec(value.shape, at) for at, value in enumerate(operands)]
            + [pl.BlockSpec(memory_space=pl.ANY)] * len(earlier),
            out_specs=[spec(shape, count + at) for at, (shape, _) in enumerate(outs)],
            scratch_shapes=list(scratch),
            input_output_aliases={0: 0} if alias else {},
            compiler_params=pltpu.CompilerParams(vmem_limit_bytes=VMEM_LIMIT),
            cost_estimate=pl.CostEstimate(flops=flops, bytes_accessed=0, transcendentals=0),
        )(*operands, *earlier)
        self.last = (made[key],)
        return made


def blocks_of(rows, size=256):
    def run(body):
        def step(index, carry):
            body(pl.ds(pl.multiple_of(index * size, size), size))
            return carry

        lax.fori_loop(0, rows // size, step, 0)

    return run


def dot(left, right):
    return jnp.dot(left, right, preferred_element_type=jnp.float32)


class Layout:
    def __init__(self, mesh_shape, rows):
        seq, self.sub = mesh_shape["seq"], mesh_shape["sub"]
        self.count = seq * self.sub
        self.plane = DILATION_STEP // rows
        self.blocks = self.plane // 2
        self.ring = self.count // self.plane
        self.bins = rows * self.count

    def around(self, value, steps):
        hop = steps * self.plane
        pairs = [(i, (i + hop) % self.count) for i in range(self.count)]
        return lax.ppermute(value, AXES, pairs)

    def across(self, value, mask):
        return lax.ppermute(value, AXES, [(i, i ^ mask) for i in range(self.count)])

    def along(self, value, mask):
        return self.across(value, mask * self.plane)

    def place(self):
        flat = lax.axis_index("seq") * self.sub + lax.axis_index("sub")
        return flat & 1, lax.div(flat & (self.plane - 1), 2)


LANES, EXTRA = 128, 8


class Sum:
    def __init__(self, layout, channels, units, has_exact=False):
        self.layout, self.channels, self.units = layout, channels, units
        self.part = channels // layout.plane
        self.rows = self.part * units
        self.extra = EXTRA * has_exact
        self.held_type = ((layout.blocks, self.rows + self.extra, LANES), F32)
        self.sent_type = ((self.rows + 2 * self.extra, LANES), BF16)

    def store(self, ref, at, value):
        rows = self.rows
        if not self.extra:
            ref[at] = value.astype(BF16)
            return
        ref[at + (slice(0, rows),)] = value[:rows].astype(BF16)
        high = value[rows:].astype(BF16)
        low = (value[rows:] - high.astype(F32)).astype(BF16)
        ref[at + (slice(rows, None),)] = jnp.concatenate([high, low], axis=0)

    def load(self, value):
        value = value.astype(F32)
        if not self.extra:
            return value
        rows = self.rows
        exact = value[rows : rows + EXTRA] + value[rows + EXTRA :]
        return jnp.concatenate([value[:rows], exact], axis=0)

    def split(self, tall, wide, exact, held, away):
        core, _ = self.layout.place()
        part, plane = self.part, self.layout.plane
        thin = LANES // plane

        for block in range(self.layout.blocks):
            for mine in (True, False):
                piece = 2 * block + (core if mine else 1 - core)
                at = 0
                chunks = []
                for ref in tall:
                    for low in range(0, ref.shape[1], LANES):
                        chunks.append(ref[pl.ds(pl.multiple_of(piece * part, 8), part), low : low + LANES])
                for ref in wide:
                    for top in range(0, ref.shape[0], LANES):
                        for low in range(0, self.channels, LANES):
                            chunks.append(
                                ref[pl.ds(pl.multiple_of(top + piece * thin, 8), thin), low : low + LANES]
                            )
                if self.extra:
                    chunks.append(exact[pl.ds(pl.multiple_of(piece * EXTRA, 8), EXTRA), :])
                for value in chunks:
                    size = value.shape[0]
                    if mine:
                        held[block, at : at + size, :] = value
                    elif at < self.rows:
                        away[block, at : at + size, :] = value.astype(BF16)
                    else:
                        high = value.astype(BF16)
                        low = (value - high.astype(F32)).astype(BF16)
                        away[block, at : at + 2 * size, :] = jnp.concatenate([high, low], axis=0)
                    at += size


def sent_rows(sums):
    return sum(group.sent_type[0][0] for group in sums)


def over_plane(chain, layout, sums, halves):
    blocks, rows = layout.blocks, sent_rows(sums)

    def run(*refs):
        inputs, own, sent = refs[: 2 * len(sums)], refs[2 * len(sums)], refs[2 * len(sums) + 1 :]
        _, block = layout.place()
        top = base = 0
        for group, held, away in zip(sums, inputs[::2], inputs[1::2]):
            size, mine = group.sent_type[0][0], group.held_type[0][1]
            own[base : base + mine, :] = held[block] + group.load(away[block])
            for k in range(1, blocks):
                there = block ^ k
                group.store(sent[k - 1].at[top : top + size], (), held[there] + group.load(away[there]))
            top, base = top + size, base + mine

    mine = sum(group.held_type[0][1] for group in sums)
    outs = [((mine, LANES), F32)] + [((rows, LANES), BF16)] * (blocks - 1)
    own, *sent = chain.call(run, outs, [ref for pair in halves for ref in pair])
    arrived = {k: layout.across(sent[k - 1], 2 * k) for k in range(blocks - 1, 0, -1)}
    return [own] + [arrived[k] for k in range(1, blocks)]


def plane_sum(chain, layout, sums, parts, flops=0):
    def run(own, *refs):
        away, out = refs[:-1], refs[-1]
        top = base = 0
        for group in sums:
            size, mine = group.sent_type[0][0], group.held_type[0][1]
            value = own[base : base + mine, :]
            for ref in away:
                value = value + group.load(ref[top : top + size, :])
            group.store(out.at[top : top + size], (), value)
            top, base = top + size, base + mine

    return chain.call(run, [((sent_rows(sums), LANES), BF16)], parts, flops=flops)[0]


def pair_sum(chain, sums, mine, arrived, flops=0):
    def run(left, right, out):
        top = 0
        for group in sums:
            size = group.sent_type[0][0]
            value = group.load(left[top : top + size, :]) + group.load(right[top : top + size, :])
            group.store(out.at[top : top + size], (), value)
            top += size

    return chain.call(run, [(mine.shape, BF16)], (mine, arrived), flops=flops)[0]


def back_plane(layout, sent):
    arrived = {k: layout.across(sent, 2 * k) for k in range(layout.blocks - 1, 0, -1)}
    return [sent] + [arrived[k] for k in range(1, layout.blocks)]


def back_core(chain, layout, parts, flops=0):
    def run(*refs):
        for at, ref in enumerate(refs[:-1]):
            refs[-1][at] = ref[...]

    (own,) = chain.call(run, [((len(parts),) + parts[0].shape, BF16)], parts, flops=flops)
    return own, layout.across(own, 1)


def unsplit(layout, sums, refs, tall, wide, exact):
    core, block = layout.place()
    for at in range(2 * layout.blocks):
        other, k = divmod(at, layout.blocks)
        ref = refs[other].at[k]
        piece = 2 * (block ^ k) + (core ^ other)
        top = 0
        for number, group in enumerate(sums):
            part = group.part
            for target, low in tall[number]:
                target[pl.ds(pl.multiple_of(piece * part, 8), part), low : low + LANES] = ref[
                    top : top + part, :
                ].astype(F32)
                top += part
            thin = LANES // layout.plane
            for target, upper in wide[number]:
                for low in range(0, group.channels, LANES):
                    target[pl.ds(pl.multiple_of(upper + piece * thin, 8), thin), low : low + LANES] = ref[
                        top : top + thin, :
                    ].astype(F32)
                    top += thin
            if group.extra:
                value = ref[top : top + 2 * EXTRA, :].astype(F32)
                exact[pl.ds(pl.multiple_of(piece * EXTRA, 8), EXTRA), :] = value[:EXTRA] + value[EXTRA:]
                top += 2 * EXTRA


def solution(mesh):
    mesh_shape = dict(mesh.shape)

    def local(features, kernel, offsets, mixer, biases, cotangent):
        rows, channels = features.shape
        width = kernel.shape[2]
        layout = Layout(mesh_shape, rows)
        factor = 1.0 / math.sqrt(layout.bins)
        plane = layout.plane
        cuts = [(0, LANES), (LANES, width)]
        chain = Chain()

        def activate(source, activated):
            @blocks_of(rows)
            def _(block):
                activated[block, :] = gelu_parts(source[block, :].astype(F32))[0].astype(BF16)

        (activated,) = chain.call(activate, [((rows, channels), BF16)], (features,))

        def forward_tap(active, weights, out):
            @blocks_of(rows)
            def _(block):
                out[block, :] = dot(active[block, :], weights[0]).astype(BF16)

        outs = [((rows, width), BF16)]
        (early,) = chain.call(forward_tap, outs, (activated, kernel), tap=0)
        (late,) = chain.call(forward_tap, outs, (activated, kernel), tap=2, flops=LONG)
        early, late = layout.around(early, 1), layout.around(late, -1)

        def local_parts(active, weights, shift, cot, mix, center, hidden_grad):
            @blocks_of(rows)
            def _(block):
                center[block, :] = dot(active[block, :], weights[1]) + shift[...]
                hidden_grad[block, :] = times_transposed(cot[block, :], mix[...])

        center, hidden_grad = chain.call(
            local_parts,
            [((rows, width), F32)] * 2,
            (activated, kernel, offsets.reshape(1, width), cotangent, mixer),
        )

        def own_grads(low, high):
            def run(center, hidden_grad, early, late, hidden, grad):
                @blocks_of(rows)
                def _(block):
                    preact = (
                        center[block, low:high]
                        + early[block, low:high].astype(F32)
                        + late[block, low:high].astype(F32)
                    )
                    value, slope = gelu_parts(preact)
                    hidden[block, :] = value.astype(BF16)
                    grad[block, :] = (hidden_grad[block, low:high] * slope).astype(BF16)

            return run

        hidden, grads, arrived = [], [], []
        for low, high in cuts:
            outs = [((rows, high - low), BF16)] * 2
            value, grad = chain.call(own_grads(low, high), outs, (center, hidden_grad, early, late))
            hidden.append(value)
            grads.append(grad)
            arrived.append((layout.around(grad, -1), layout.around(grad, 1)))

        count = len(cuts)

        def vector_sums(cot, *refs):
            grads, out = refs[:-1], refs[-1]
            sources = [(cot, low) for low in range(0, channels, LANES)]
            sources += [(ref, low) for ref in grads for low in range(0, ref.shape[1], LANES)]
            out[...] = jnp.zeros_like(out)
            for row, (ref, low) in enumerate(sources):
                value = ref[:, low : low + LANES].astype(F32)
                out[row : row + 1, :] = jnp.sum(value, axis=0, keepdims=True) * factor

        (vectors,) = chain.call(vector_sums, [((plane * EXTRA, LANES), F32)], (cotangent, *grads))

        def split_types(group):
            shape, _ = group.held_type
            return [group.held_type, (shape[:1] + group.sent_type[0], BF16)]

        def own_weights(active, cot, exact, *refs):
            hidden, grads = refs[:count], refs[count : 2 * count]
            held, away, tall, wide = refs[2 * count :]
            for (low, high), value, grad in zip(cuts, hidden, grads):
                tall[:, low:high] = contract_rows(active[...], grad[...]) * factor
                wide[low:high, :] = contract_rows(value[...], cot[...]) * factor
            own.split([tall], [wide], exact, held, away)

        own = Sum(layout, channels, 2 * width // LANES, True)
        held, away = chain.call(
            own_weights,
            split_types(own),
            (activated, cotangent, vectors, *hidden, *grads),
            [pltpu.VMEM((channels, width), F32), pltpu.VMEM((width, channels), F32)],
        )

        own_half = (held, layout.across(away, 1))

        def output_parts(source, mix, shift, weights, *refs):
            hidden, grads = refs[:count], refs[count : 2 * count]
            output, product = refs[2 * count :]

            @blocks_of(rows)
            def _(block):
                total = source[block, :].astype(F32) + shift[...]
                back = jnp.zeros((total.shape[0], channels), F32)
                for (low, high), value, grad in zip(cuts, hidden, grads):
                    total = total + dot(value[block, :], mix[low:high, :])
                    back = back + times_transposed(grad[block, :], weights[1, :, low:high])
                output[block, :] = total.astype(BF16)
                product[block, :] = back

        layer_output, product = chain.call(
            output_parts,
            [((rows, channels), BF16), ((rows, channels), F32)],
            (features, mixer, biases.reshape(1, channels), kernel, *hidden, *grads),
            flops=LONG,
            key=1,
        )

        def side_weights(group, low, high):
            def run(active, later, earlier, held, away, first, second):
                first[...] = contract_rows(active[...], later[...]) * factor
                second[...] = contract_rows(active[...], earlier[...]) * factor
                group.split([first, second], [], None, held, away)

            return run

        def side_product(product, later, earlier, weights, out):
            low, high = cuts[0]

            @blocks_of(rows)
            def _(block):
                out[block, :] = (
                    product[block, :]
                    + times_transposed(later[block, :], weights[0, :, low:high])
                    + times_transposed(earlier[block, :], weights[2, :, low:high])
                )

        def input_grads(product, later, earlier, weights, cot, slope, out, done):
            low, high = cuts[1]
            done[...] = jnp.zeros_like(done)

            @blocks_of(rows)
            def _(block):
                total = (
                    product[block, :]
                    + times_transposed(later[block, :], weights[0, :, low:high])
                    + times_transposed(earlier[block, :], weights[2, :, low:high])
                )
                out[block, :] = (cot[block, :].astype(F32) + total * slope[block, :]).astype(BF16)

        side_sums = [Sum(layout, channels, 2 * (high - low) // LANES) for low, high in cuts]

        FLOPS = (LONG, LONG)

        def start_side(at):
            low, high = cuts[at]
            return chain.call(
                side_weights(side_sums[at], low, high),
                split_types(side_sums[at]),
                (activated, *arrived[at]),
                [pltpu.VMEM((channels, high - low), F32)] * 2,
                FLOPS[at],
            )

        def input_slope(source, slope):
            @blocks_of(rows)
            def _(block):
                slope[block, :] = gelu_parts(source[block, :].astype(F32))[1]


        held, away = start_side(0)
        halves = [own_half, (held, layout.across(away, 1))]
        (product,) = chain.call(
            side_product,
            [((rows, channels), F32)],
            (product, *arrived[0], kernel),
            flops=LONG,
        )
        first_sums, last_sums = [own, side_sums[0]], side_sums[1:]
        parts = over_plane(chain, layout, first_sums, halves)
        (slope_in,) = chain.call(input_slope, [((rows, channels), F32)], (features,), flops=LONG)
        first_sent = plane_sum(chain, layout, first_sums, parts, LONG)
        masks = [1 << bit for bit in range(layout.ring.bit_length() - 1)]
        first_arrived = layout.along(first_sent, masks[0])

        held, away = start_side(1)
        halves = [(held, layout.across(away, 1))]
        for mask in masks[1:]:
            first_sent = pair_sum(chain, first_sums, first_sent, first_arrived, LONG)
            first_arrived = layout.along(first_sent, mask)
        parts = over_plane(chain, layout, last_sums, halves)
        last_sent = plane_sum(chain, layout, last_sums, parts)
        last_arrived = layout.along(last_sent, masks[0])
        first_level = back_plane(layout, pair_sum(chain, first_sums, first_sent, first_arrived))
        for mask in masks[1:]:
            last_sent = pair_sum(chain, last_sums, last_sent, last_arrived)
            last_arrived = layout.along(last_sent, mask)
        input_grad, _ = chain.call(
            input_grads,
            [((rows, channels), BF16), ((8, LANES), F32)],
            (product, *arrived[1], kernel, cotangent, slope_in),
            flops=LONG,
            key=1,
        )
        last_sent = pair_sum(chain, last_sums, last_sent, last_arrived)
        last_level = back_plane(layout, last_sent)
        first_level = back_core(chain, layout, first_level, LONG)
        last_level = back_core(chain, layout, last_level, LONG)

        def side_targets(kernel_grad, low, high):
            return [(kernel_grad.at[i], at) for i in (0, 2) for at in range(low, high, LANES)]

        def finish_first(*refs):
            arrived, refs = refs[:2], refs[2:]
            kernel_grad, mixer_grad, biases_grad, offset_grad = refs[:4]
            center, sides, exact, sems = refs[4:]
            targets = range(0, width, LANES)
            low, high = cuts[0]
            unsplit(
                layout,
                first_sums,
                arrived,
                [
                    [(center, at) for at in targets],
                    [(sides.at[i], at) for i in (0, 1) for at in range(0, high - low, LANES)],
                ],
                [[(mixer_grad, at) for at in targets], []],
                exact,
            )
            copies = [pltpu.make_async_copy(center, kernel_grad.at[1], sems.at[0])]
            for i in (0, 1):
                copies.append(
                    pltpu.make_async_copy(
                        sides.at[i], kernel_grad.at[2 * i, :, low:high], sems.at[1 + i]
                    )
                )
            for copy in copies:
                copy.start()
            for at in range(0, channels, LANES):
                biases_grad[at : at + LANES] = exact[at // LANES, :]
            for at in range(0, width, LANES):
                offset_grad[at : at + LANES] = exact[(channels + at) // LANES, :]
            for copy in copies:
                copy.wait()

        low, high = cuts[0]
        kernel_grad, mixer_grad, biases_grad, offset_grad = chain.call(
            finish_first,
            [
                ((3, channels, width), F32),
                ((width, channels), F32),
                ((channels,), F32),
                ((width,), F32),
            ],
            first_level,
            [
                pltpu.VMEM((channels, width), F32),
                pltpu.VMEM((2, channels, high - low), F32),
                pltpu.VMEM((plane * EXTRA, LANES), F32),
                pltpu.SemaphoreType.DMA((3,)),
            ],
            far=(2,),
            key=3,
        )

        def finish_last(begun, *refs):
            arrived, (kernel_grad, sides, sems) = refs[:2], refs[2:]
            low, high = cuts[1]
            unsplit(
                layout,
                last_sums,
                arrived,
                [[(sides.at[i], at) for i in (0, 1) for at in range(0, high - low, LANES)]],
                [[]],
                None,
            )
            copies = [
                pltpu.make_async_copy(sides.at[i], kernel_grad.at[2 * i, :, low:high], sems.at[i])
                for i in (0, 1)
            ]
            for copy in copies:
                copy.start()
            for copy in copies:
                copy.wait()

        low, high = cuts[1]
        chain.last = ()
        (kernel_grad,) = chain.call(
            finish_last,
            [((3, channels, width), F32)],
            (kernel_grad, *last_level),
            [pltpu.VMEM((2, channels, high - low), F32), pltpu.SemaphoreType.DMA((2,))],
            far=(0, 3),
            alias=True,
        )
        return (
            layer_output,
            input_grad,
            kernel_grad,
            offset_grad,
            mixer_grad,
            biases_grad,
        )

    rows_split = P(AXES, None)
    return jax.shard_map(
        local,
        mesh=mesh,
        in_specs=(rows_split, P(), P(), P(), P(), rows_split),
        out_specs=(rows_split, rows_split, P(), P(), P(), P()),
        check_vma=False,
    )
```

```python
import math

import jax
import jax.numpy as jnp
from jax import lax
from jax.experimental import pallas as pl
from jax.experimental.pallas import tpu as pltpu
from jax.sharding import PartitionSpec as P

DILATION_STEP = 8192
AXES = ("seq", "sub")
VMEM_LIMIT = 16 * 1024 * 1024
LONG = 8 * 10**9
BF16, F32 = jnp.bfloat16, jnp.float32


def gelu_parts(values):
    normal_cdf = 0.5 * (1.0 + lax.erf(values * (1.0 / math.sqrt(2.0))))
    slope = normal_cdf + values * jnp.exp(-0.5 * values * values) * (1.0 / math.sqrt(2.0 * math.pi))
    return values * normal_cdf, slope


def contract_rows(left, right):
    return lax.dot_general(
        left, right, (((0,), (0,)), ((), ())), preferred_element_type=jnp.float32
    )


def times_transposed(left, right):
    return lax.dot_general(
        left, right, (((1,), (1,)), ((), ())), preferred_element_type=jnp.float32
    )


class Chain:
    def __init__(self):
        self.last = ()

    def call(self, body, outs, operands, scratch=(), flops=0, blocked=(), key=0, far=(), alias=False, tap=None):
        count, earlier = len(operands), self.last

        def kernel(*refs):
            body(*refs[:count], *refs[count + len(earlier) :])

        def spec(shape, at):
            if tap is not None and at == count - 1:
                return pl.BlockSpec((1,) + shape[1:], lambda _: (tap, 0, 0))
            if at in far:
                return pl.BlockSpec(memory_space=pltpu.HBM)
            if not blocked:
                return pl.BlockSpec(memory_space=pltpu.VMEM)
            if blocked[at]:
                return pl.BlockSpec((shape[0] // 4,) + shape[1:], lambda i: (i, 0))
            return pl.BlockSpec(shape, lambda i: (0,) * len(shape))

        made = pl.pallas_call(
            kernel,
            grid=(4,) if blocked else () if tap is None else (1,),
            out_shape=[jax.ShapeDtypeStruct(shape, dtype) for shape, dtype in outs],
            in_specs=[spec(value.shape, at) for at, value in enumerate(operands)]
            + [pl.BlockSpec(memory_space=pl.ANY)] * len(earlier),
            out_specs=[spec(shape, count + at) for at, (shape, _) in enumerate(outs)],
            scratch_shapes=list(scratch),
            input_output_aliases={0: 0} if alias else {},
            compiler_params=pltpu.CompilerParams(vmem_limit_bytes=VMEM_LIMIT),
            cost_estimate=pl.CostEstimate(flops=flops, bytes_accessed=0, transcendentals=0),
        )(*operands, *earlier)
        self.last = (made[key],)
        return made


def blocks_of(rows, size=256):
    def run(body):
        def step(index, carry):
            body(pl.ds(pl.multiple_of(index * size, size), size))
            return carry

        lax.fori_loop(0, rows // size, step, 0)

    return run


def dot(left, right):
    return jnp.dot(left, right, preferred_element_type=jnp.float32)


class Layout:
    def __init__(self, mesh_shape, rows):
        seq, self.sub = mesh_shape["seq"], mesh_shape["sub"]
        self.count = seq * self.sub
        self.plane = DILATION_STEP // rows
        self.blocks = self.plane // 2
        self.ring = self.count // self.plane
        self.bins = rows * self.count

    def around(self, value, steps):
        hop = steps * self.plane
        pairs = [(i, (i + hop) % self.count) for i in range(self.count)]
        return lax.ppermute(value, AXES, pairs)

    def across(self, value, mask):
        return lax.ppermute(value, AXES, [(i, i ^ mask) for i in range(self.count)])

    def along(self, value, mask):
        return self.across(value, mask * self.plane)

    def place(self):
        flat = lax.axis_index("seq") * self.sub + lax.axis_index("sub")
        return flat & 1, lax.div(flat & (self.plane - 1), 2)


LANES, EXTRA = 128, 8


class Sum:
    def __init__(self, layout, channels, units, has_exact=False):
        self.layout, self.channels, self.units = layout, channels, units
        self.part = channels // layout.plane
        self.rows = self.part * units
        self.extra = EXTRA * has_exact
        self.held_type = ((layout.blocks, self.rows + self.extra, LANES), F32)
        self.sent_type = ((self.rows + 2 * self.extra, LANES), BF16)

    def store(self, ref, at, value):
        rows = self.rows
        if not self.extra:
            ref[at] = value.astype(BF16)
            return
        ref[at + (slice(0, rows),)] = value[:rows].astype(BF16)
        high = value[rows:].astype(BF16)
        low = (value[rows:] - high.astype(F32)).astype(BF16)
        ref[at + (slice(rows, None),)] = jnp.concatenate([high, low], axis=0)

    def load(self, value):
        value = value.astype(F32)
        if not self.extra:
            return value
        rows = self.rows
        exact = value[rows : rows + EXTRA] + value[rows + EXTRA :]
        return jnp.concatenate([value[:rows], exact], axis=0)

    def split(self, tall, wide, exact, held, away):
        core, _ = self.layout.place()
        part, plane = self.part, self.layout.plane
        thin = LANES // plane

        for block in range(self.layout.blocks):
            for mine in (True, False):
                piece = 2 * block + (core if mine else 1 - core)
                at = 0
                chunks = []
                for ref in tall:
                    for low in range(0, ref.shape[1], LANES):
                        chunks.append(ref[pl.ds(pl.multiple_of(piece * part, 8), part), low : low + LANES])
                for ref in wide:
                    for top in range(0, ref.shape[0], LANES):
                        for low in range(0, self.channels, LANES):
                            chunks.append(
                                ref[pl.ds(pl.multiple_of(top + piece * thin, 8), thin), low : low + LANES]
                            )
                if self.extra:
                    chunks.append(exact[pl.ds(pl.multiple_of(piece * EXTRA, 8), EXTRA), :])
                for value in chunks:
                    size = value.shape[0]
                    if mine:
                        held[block, at : at + size, :] = value
                    elif at < self.rows:
                        away[block, at : at + size, :] = value.astype(BF16)
                    else:
                        high = value.astype(BF16)
                        low = (value - high.astype(F32)).astype(BF16)
                        away[block, at : at + 2 * size, :] = jnp.concatenate([high, low], axis=0)
                    at += size


def sent_rows(sums):
    return sum(group.sent_type[0][0] for group in sums)


def over_plane(chain, layout, sums, halves):
    blocks, rows = layout.blocks, sent_rows(sums)

    def run(*refs):
        inputs, own, sent = refs[: 2 * len(sums)], refs[2 * len(sums)], refs[2 * len(sums) + 1 :]
        _, block = layout.place()
        top = base = 0
        for group, held, away in zip(sums, inputs[::2], inputs[1::2]):
            size, mine = group.sent_type[0][0], group.held_type[0][1]
            own[base : base + mine, :] = held[block] + group.load(away[block])
            for k in range(1, blocks):
                there = block ^ k
                group.store(sent[k - 1].at[top : top + size], (), held[there] + group.load(away[there]))
            top, base = top + size, base + mine

    mine = sum(group.held_type[0][1] for group in sums)
    outs = [((mine, LANES), F32)] + [((rows, LANES), BF16)] * (blocks - 1)
    own, *sent = chain.call(run, outs, [ref for pair in halves for ref in pair])
    arrived = {k: layout.across(sent[k - 1], 2 * k) for k in range(blocks - 1, 0, -1)}
    return [own] + [arrived[k] for k in range(1, blocks)]


def plane_sum(chain, layout, sums, parts, flops=0):
    def run(own, *refs):
        away, out = refs[:-1], refs[-1]
        top = base = 0
        for group in sums:
            size, mine = group.sent_type[0][0], group.held_type[0][1]
            value = own[base : base + mine, :]
            for ref in away:
                value = value + group.load(ref[top : top + size, :])
            group.store(out.at[top : top + size], (), value)
            top, base = top + size, base + mine

    return chain.call(run, [((sent_rows(sums), LANES), BF16)], parts, flops=flops)[0]


def pair_sum(chain, sums, mine, arrived, flops=0):
    def run(left, right, out):
        top = 0
        for group in sums:
            size = group.sent_type[0][0]
            value = group.load(left[top : top + size, :]) + group.load(right[top : top + size, :])
            group.store(out.at[top : top + size], (), value)
            top += size

    return chain.call(run, [(mine.shape, BF16)], (mine, arrived), flops=flops)[0]


def back_plane(layout, sent):
    arrived = {k: layout.across(sent, 2 * k) for k in range(layout.blocks - 1, 0, -1)}
    return [sent] + [arrived[k] for k in range(1, layout.blocks)]


def back_core(chain, layout, parts, flops=0):
    def run(*refs):
        for at, ref in enumerate(refs[:-1]):
            refs[-1][at] = ref[...]

    (own,) = chain.call(run, [((len(parts),) + parts[0].shape, BF16)], parts, flops=flops)
    return own, layout.across(own, 1)


def unsplit(layout, sums, refs, tall, wide, exact):
    core, block = layout.place()
    for at in range(2 * layout.blocks):
        other, k = divmod(at, layout.blocks)
        ref = refs[other].at[k]
        piece = 2 * (block ^ k) + (core ^ other)
        top = 0
        for number, group in enumerate(sums):
            part = group.part
            for target, low in tall[number]:
                target[pl.ds(pl.multiple_of(piece * part, 8), part), low : low + LANES] = ref[
                    top : top + part, :
                ].astype(F32)
                top += part
            thin = LANES // layout.plane
            for target, upper in wide[number]:
                for low in range(0, group.channels, LANES):
                    target[pl.ds(pl.multiple_of(upper + piece * thin, 8), thin), low : low + LANES] = ref[
                        top : top + thin, :
                    ].astype(F32)
                    top += thin
            if group.extra:
                value = ref[top : top + 2 * EXTRA, :].astype(F32)
                exact[pl.ds(pl.multiple_of(piece * EXTRA, 8), EXTRA), :] = value[:EXTRA] + value[EXTRA:]
                top += 2 * EXTRA


def solution(mesh):
    mesh_shape = dict(mesh.shape)

    def local(features, kernel, offsets, mixer, biases, cotangent):
        rows, channels = features.shape
        width = kernel.shape[2]
        layout = Layout(mesh_shape, rows)
        factor = 1.0 / math.sqrt(layout.bins)
        plane = layout.plane
        cuts = [(0, LANES), (LANES, width)]
        chain = Chain()

        def activate_and_tap(source, weights, out, activated):
            active = gelu_parts(source[...].astype(F32))[0].astype(BF16)
            activated[...] = active
            out[...] = dot(active, weights[0]).astype(BF16)

        early, activated = chain.call(
            activate_and_tap,
            [((rows, width), BF16), ((rows, channels), BF16)],
            (features, kernel),
            blocked=(1, 0, 1, 1),
            tap=0,
        )

        def forward_tap(active, weights, out):
            @blocks_of(rows)
            def _(block):
                out[block, :] = dot(active[block, :], weights[0]).astype(BF16)

        outs = [((rows, width), BF16)]
        (late,) = chain.call(forward_tap, outs, (activated, kernel), tap=2, flops=LONG)
        early, late = layout.around(early, 1), layout.around(late, -1)

        def local_parts(active, weights, shift, cot, mix, center, hidden_grad):
            @blocks_of(rows)
            def _(block):
                center[block, :] = dot(active[block, :], weights[1]) + shift[...]
                hidden_grad[block, :] = times_transposed(cot[block, :], mix[...])

        center, hidden_grad = chain.call(
            local_parts,
            [((rows, width), F32)] * 2,
            (activated, kernel, offsets.reshape(1, width), cotangent, mixer),
        )

        def own_grads(low, high):
            def run(center, hidden_grad, early, late, hidden, grad):
                @blocks_of(rows)
                def _(block):
                    preact = (
                        center[block, low:high]
                        + early[block, low:high].astype(F32)
                        + late[block, low:high].astype(F32)
                    )
                    value, slope = gelu_parts(preact)
                    hidden[block, :] = value.astype(BF16)
                    grad[block, :] = (hidden_grad[block, low:high] * slope).astype(BF16)

            return run

        hidden, grads, arrived = [], [], []
        for low, high in cuts:
            outs = [((rows, high - low), BF16)] * 2
            value, grad = chain.call(own_grads(low, high), outs, (center, hidden_grad, early, late))
            hidden.append(value)
            grads.append(grad)
            arrived.append((layout.around(grad, -1), layout.around(grad, 1)))

        count = len(cuts)

        def vector_sums(cot, *refs):
            grads, out = refs[:-1], refs[-1]
            sources = [(cot, low) for low in range(0, channels, LANES)]
            sources += [(ref, low) for ref in grads for low in range(0, ref.shape[1], LANES)]
            out[...] = jnp.zeros_like(out)
            for row, (ref, low) in enumerate(sources):
                value = ref[:, low : low + LANES].astype(F32)
                out[row : row + 1, :] = jnp.sum(value, axis=0, keepdims=True) * factor

        (vectors,) = chain.call(vector_sums, [((plane * EXTRA, LANES), F32)], (cotangent, *grads))

        def split_types(group):
            shape, _ = group.held_type
            return [group.held_type, (shape[:1] + group.sent_type[0], BF16)]

        def own_weights(active, cot, exact, *refs):
            hidden, grads = refs[:count], refs[count : 2 * count]
            held, away, tall, wide = refs[2 * count :]
            for (low, high), value, grad in zip(cuts, hidden, grads):
                tall[:, low:high] = contract_rows(active[...], grad[...]) * factor
                wide[low:high, :] = contract_rows(value[...], cot[...]) * factor
            own.split([tall], [wide], exact, held, away)

        own = Sum(layout, channels, 2 * width // LANES, True)
        held, away = chain.call(
            own_weights,
            split_types(own),
            (activated, cotangent, vectors, *hidden, *grads),
            [pltpu.VMEM((channels, width), F32), pltpu.VMEM((width, channels), F32)],
        )

        own_half = (held, layout.across(away, 1))

        def output_parts(source, mix, shift, weights, *refs):
            hidden, grads = refs[:count], refs[count : 2 * count]
            output, product = refs[2 * count :]

            @blocks_of(rows)
            def _(block):
                total = source[block, :].astype(F32) + shift[...]
                back = jnp.zeros((total.shape[0], channels), F32)
                for (low, high), value, grad in zip(cuts, hidden, grads):
                    total = total + dot(value[block, :], mix[low:high, :])
                    back = back + times_transposed(grad[block, :], weights[1, :, low:high])
                output[block, :] = total.astype(BF16)
                product[block, :] = back

        layer_output, product = chain.call(
            output_parts,
            [((rows, channels), BF16), ((rows, channels), F32)],
            (features, mixer, biases.reshape(1, channels), kernel, *hidden, *grads),
            flops=LONG,
            key=1,
        )

        def side_weights(group, low, high):
            def run(active, later, earlier, held, away, first, second):
                first[...] = contract_rows(active[...], later[...]) * factor
                second[...] = contract_rows(active[...], earlier[...]) * factor
                group.split([first, second], [], None, held, away)

            return run

        def side_product(product, later, earlier, weights, out):
            low, high = cuts[0]

            @blocks_of(rows)
            def _(block):
                out[block, :] = (
                    product[block, :]
                    + times_transposed(later[block, :], weights[0, :, low:high])
                    + times_transposed(earlier[block, :], weights[2, :, low:high])
                )

        def input_grads(product, later, earlier, weights, cot, slope, out, done):
            low, high = cuts[1]
            done[...] = jnp.zeros_like(done)

            @blocks_of(rows)
            def _(block):
                total = (
                    product[block, :]
                    + times_transposed(later[block, :], weights[0, :, low:high])
                    + times_transposed(earlier[block, :], weights[2, :, low:high])
                )
                out[block, :] = (cot[block, :].astype(F32) + total * slope[block, :]).astype(BF16)

        side_sums = [Sum(layout, channels, 2 * (high - low) // LANES) for low, high in cuts]

        FLOPS = (LONG, LONG)

        def start_side(at):
            low, high = cuts[at]
            return chain.call(
                side_weights(side_sums[at], low, high),
                split_types(side_sums[at]),
                (activated, *arrived[at]),
                [pltpu.VMEM((channels, high - low), F32)] * 2,
                FLOPS[at],
            )

        def input_slope(source, slope):
            @blocks_of(rows)
            def _(block):
                slope[block, :] = gelu_parts(source[block, :].astype(F32))[1]


        held, away = start_side(0)
        halves = [own_half, (held, layout.across(away, 1))]
        (product,) = chain.call(
            side_product,
            [((rows, channels), F32)],
            (product, *arrived[0], kernel),
            flops=LONG,
        )
        first_sums, last_sums = [own, side_sums[0]], side_sums[1:]
        parts = over_plane(chain, layout, first_sums, halves)
        (slope_in,) = chain.call(input_slope, [((rows, channels), F32)], (features,), flops=LONG)
        first_sent = plane_sum(chain, layout, first_sums, parts, LONG)
        masks = [1 << bit for bit in range(layout.ring.bit_length() - 1)]
        first_arrived = layout.along(first_sent, masks[0])

        held, away = start_side(1)
        halves = [(held, layout.across(away, 1))]
        for mask in masks[1:]:
            first_sent = pair_sum(chain, first_sums, first_sent, first_arrived, LONG)
            first_arrived = layout.along(first_sent, mask)
        parts = over_plane(chain, layout, last_sums, halves)
        last_sent = plane_sum(chain, layout, last_sums, parts)
        last_arrived = layout.along(last_sent, masks[0])
        first_level = back_plane(layout, pair_sum(chain, first_sums, first_sent, first_arrived))
        for mask in masks[1:]:
            last_sent = pair_sum(chain, last_sums, last_sent, last_arrived)
            last_arrived = layout.along(last_sent, mask)
        input_grad, _ = chain.call(
            input_grads,
            [((rows, channels), BF16), ((8, LANES), F32)],
            (product, *arrived[1], kernel, cotangent, slope_in),
            flops=LONG,
            key=1,
        )
        last_sent = pair_sum(chain, last_sums, last_sent, last_arrived)
        last_level = back_plane(layout, last_sent)
        first_level = back_core(chain, layout, first_level, LONG)
        last_level = back_core(chain, layout, last_level, LONG)

        def side_targets(kernel_grad, low, high):
            return [(kernel_grad.at[i], at) for i in (0, 2) for at in range(low, high, LANES)]

        def finish_first(*refs):
            arrived, refs = refs[:2], refs[2:]
            kernel_grad, mixer_grad, biases_grad, offset_grad = refs[:4]
            center, sides, exact, sems = refs[4:]
            targets = range(0, width, LANES)
            low, high = cuts[0]
            unsplit(
                layout,
                first_sums,
                arrived,
                [
                    [(center, at) for at in targets],
                    [(sides.at[i], at) for i in (0, 1) for at in range(0, high - low, LANES)],
                ],
                [[(mixer_grad, at) for at in targets], []],
                exact,
            )
            copies = [pltpu.make_async_copy(center, kernel_grad.at[1], sems.at[0])]
            for i in (0, 1):
                copies.append(
                    pltpu.make_async_copy(
                        sides.at[i], kernel_grad.at[2 * i, :, low:high], sems.at[1 + i]
                    )
                )
            for copy in copies:
                copy.start()
            for at in range(0, channels, LANES):
                biases_grad[at : at + LANES] = exact[at // LANES, :]
            for at in range(0, width, LANES):
                offset_grad[at : at + LANES] = exact[(channels + at) // LANES, :]
            for copy in copies:
                copy.wait()

        low, high = cuts[0]
        kernel_grad, mixer_grad, biases_grad, offset_grad = chain.call(
            finish_first,
            [
                ((3, channels, width), F32),
                ((width, channels), F32),
                ((channels,), F32),
                ((width,), F32),
            ],
            first_level,
            [
                pltpu.VMEM((channels, width), F32),
                pltpu.VMEM((2, channels, high - low), F32),
                pltpu.VMEM((plane * EXTRA, LANES), F32),
                pltpu.SemaphoreType.DMA((3,)),
            ],
            far=(2,),
            key=3,
        )

        def finish_last(begun, *refs):
            arrived, (kernel_grad, sides, sems) = refs[:2], refs[2:]
            low, high = cuts[1]
            unsplit(
                layout,
                last_sums,
                arrived,
                [[(sides.at[i], at) for i in (0, 1) for at in range(0, high - low, LANES)]],
                [[]],
                None,
            )
            copies = [
                pltpu.make_async_copy(sides.at[i], kernel_grad.at[2 * i, :, low:high], sems.at[i])
                for i in (0, 1)
            ]
            for copy in copies:
                copy.start()
            for copy in copies:
                copy.wait()

        low, high = cuts[1]
        chain.last = ()
        (kernel_grad,) = chain.call(
            finish_last,
            [((3, channels, width), F32)],
            (kernel_grad, *last_level),
            [pltpu.VMEM((2, channels, high - low), F32), pltpu.SemaphoreType.DMA((2,))],
            far=(0, 3),
            alias=True,
        )
        return (
            layer_output,
            input_grad,
            kernel_grad,
            offset_grad,
            mixer_grad,
            biases_grad,
        )

    rows_split = P(AXES, None)
    return jax.shard_map(
        local,
        mesh=mesh,
        in_specs=(rows_split, P(), P(), P(), P(), rows_split),
        out_specs=(rows_split, rows_split, P(), P(), P(), P()),
        check_vma=False,
    )
```
